32 devices in a mesh: replica: 4 (over x, core), shard: 8 (over z, y).
Axes of the slice: x: 2, y: 2, z: 4, core: 2. Of those that a mesh axis runs over, the one named last changes fastest.
Arguments:
- tokens: bfloat16 [32768, 768], P(('replica', 'shard')), may hold values from -6 to 6
- gain_attn: bfloat16 [768], P('shard'), may hold values from 0.099609375 to 1.8984375
- w_qkv: bfloat16 [768, 2304], P('shard'), may hold values from -0.3125 to 0.3125
- w_out: bfloat16 [768, 768], P('shard'), may hold values from -0.875 to 0.875
- gain_ffn: bfloat16 [768], P('shard'), may hold values from 0.099609375 to 1.8984375
- w_in: bfloat16 [768, 2304], P('shard'), may hold values from -0.21875 to 0.21875
- w_down: bfloat16 [1152, 768], P('shard'), may hold values from -0.1875 to 0.1875
- cotangent: bfloat16 [32768, 768], P(('replica', 'shard')), may hold values from -6 to 6
Outputs:
- output: bfloat16 [32768, 768], P(('replica', 'shard'))
- input_grad: bfloat16 [32768, 768], P(('replica', 'shard'))
- grad_gain_attn: float32 [768], P('shard')
- grad_qkv: float32 [768, 2304], P('shard')
- grad_out: float32 [768, 768], P('shard')
- grad_gain_ffn: float32 [768], P('shard')
- grad_in: float32 [768, 2304], P('shard')
- grad_down: float32 [1152, 768], P('shard')
The draws below stay inside these ranges and needn't reach their ends.
All inputs are finite; a program needn't handle non-finite values.
Results may differ from the reference program's by a relative error of at most 0.018.
Values may be sent and summed in bfloat16 or wider, within the bound.
A program may use at most 128 MiB of HBM per device.

```python
import math
import jax
import jax.numpy as jnp
from jax import lax

D = 768
HEADS = 12
HEAD_DIM = 64
FF = 1152
WINDOW = 128
LENGTH = 1024
TOKENS = 32768


def shard_levels(stream_key, shape, shards, least, largest):
    level, own = 1.0, jax.random.fold_in(stream_key, 6)
    for position, blocks in shards:
        heights = jnp.exp(jax.random.uniform(jax.random.fold_in(own, position), (blocks,), jnp.float32, least / len(shards), largest / len(shards)))
        level = level * jnp.repeat(heights, shape[position] // blocks).reshape([-1 if axis == position else 1 for axis in range(len(shape))])
    return level


def bell_draw(stream_key, dims, scale, most, cuts=(), kind=jnp.bfloat16):
    drawn = jax.random.normal(stream_key, dims, jnp.float32) * scale
    if len(cuts) > 0:
        drawn = shard_levels(stream_key, dims, cuts, -0.22, 0.18) * drawn
    return jnp.clip(drawn, min=-most, max=most).astype(kind)


def setup_inputs(seed: int = 0) -> dict:
    streams_of = jax.random.split(jax.random.key(seed), 9)
    return {
        "tokens": bell_draw(streams_of[0], (TOKENS, D), 1.0, 6.0, ((0, 32),)),
        "gain_attn": jnp.clip(1.0 + 0.18 * jax.random.normal(streams_of[1], (D,), jnp.float32), 0.099609375, 1.8984375).astype(jnp.bfloat16),
        "w_qkv": bell_draw(streams_of[2], (D, 3 * D), (D // 2) ** -0.5, 0.3125, ((0, 8),)),
        "w_out": bell_draw(streams_of[3], (D, D), (D // 16) ** -0.5, 0.875, ((0, 8),)),
        "gain_ffn": jnp.clip(1.0 + 0.18 * jax.random.normal(streams_of[4], (D,), jnp.float32), 0.099609375, 1.8984375).astype(jnp.bfloat16),
        "w_in": bell_draw(streams_of[5], (D, 2 * FF), D ** -0.5, 0.21875, ((0, 8),)),
        "w_down": bell_draw(streams_of[6], (FF, D), FF ** -0.5, 0.1875, ((0, 8),)),
        "cotangent": bell_draw(streams_of[7], (TOKENS, D), 1.0, 6.0, ((0, 32),)),
    }


@jax.custom_vjp
def low(v):
    return lax.optimization_barrier(v.astype(jnp.bfloat16)).astype(jnp.float32)

@jax.custom_vjp
def low_back(v):
    return v

def low_keep(v):
    return (low(v), None)

def low_pass(kept, grad):
    return (grad,)

def back_keep(v):
    return (v, None)

def back_low(kept, grad):
    return (low(grad),)
low.defvjp(low_keep, low_pass)
low_back.defvjp(back_keep, back_low)
epsilon = 1e-05
highest = lax.Precision.HIGHEST

def layer_norm(values, gain):
    centre = values - lax.optimization_barrier(jnp.mean(values, axis=-1, keepdims=True))
    spread = lax.optimization_barrier(jnp.mean(centre * centre, axis=-1, keepdims=True))
    return centre * lax.rsqrt(spread + epsilon) * gain

def rotary_tables(count):
    half_dim = HEAD_DIM // 2
    freqs = 10000.0 ** (-(jnp.arange(half_dim, dtype=jnp.float32) * 2.0) / HEAD_DIM)
    places = (jnp.arange(count, dtype=jnp.int32) % LENGTH).astype(jnp.float32)
    angles = places[:, None] * freqs[None, :]
    angles = jnp.concatenate([angles, angles], axis=1)
    return (jnp.cos(angles), jnp.sin(angles))

def rotate_half(values):
    half_dim = values.shape[-1] // 2
    return jnp.concatenate([-values[..., half_dim:], values[..., :half_dim]], axis=-1)

def windows(field, block_rows, margin):
    groups, length_seq = (field.shape[0], field.shape[1])
    blocks = length_seq // block_rows
    padded = jnp.pad(field, ((0, 0), (margin, block_rows - margin), (0, 0), (0, 0)))
    first = padded[:, :length_seq].reshape(groups, blocks, block_rows, HEADS, HEAD_DIM)
    second = padded[:, block_rows:block_rows + length_seq].reshape(groups, blocks, block_rows, HEADS, HEAD_DIM)
    return jnp.concatenate([first, second[:, :, :2 * margin]], axis=2)

def attention(queries, keys, values):
    groups, length_seq = (queries.shape[0], queries.shape[1])
    block_rows = min(512, length_seq)
    margin = WINDOW // 2
    blocks = length_seq // block_rows
    span = block_rows + 2 * margin
    scale = HEAD_DIM ** (-0.5)
    key_win = jnp.moveaxis(windows(keys, block_rows, margin), 1, 0)
    value_win = jnp.moveaxis(windows(values, block_rows, margin), 1, 0)
    query_blocks = jnp.moveaxis(queries.reshape(groups, blocks, block_rows, HEADS, HEAD_DIM), 1, 0)
    starts = jnp.arange(blocks, dtype=jnp.int32) * block_rows

    def one_block(pieces):
        query_part, key_part, value_part, start = pieces
        query_pos = start + jnp.arange(block_rows, dtype=jnp.int32)[:, None]
        key_pos = start - margin + jnp.arange(span, dtype=jnp.int32)[None, :]
        allowed = (key_pos >= 0) & (key_pos < length_seq) & (jnp.abs(query_pos - key_pos) <= margin)
        scores = low_back(jnp.einsum('gqhd,gkhd->ghqk', query_part, key_part, precision=highest) * scale)
        scores = jnp.where(allowed, scores, -1e+30)
        probs = low(jax.nn.softmax(scores, axis=-1))
        return jnp.einsum('ghqk,gkhd->gqhd', probs, value_part, precision=highest)
    outputs = lax.map(jax.checkpoint(one_block), (query_blocks, key_win, value_win, starts))
    return jnp.moveaxis(outputs, 0, 1).reshape(groups, length_seq, HEADS, HEAD_DIM)

def forward(stream, gain_attn, w_qkv, w_out, gain_ffn, w_in, w_down):
    groups, length_seq = (stream.shape[0], stream.shape[1])
    normed = low(layer_norm(stream, gain_attn))
    projected = low_back(jnp.einsum('gld,de->gle', normed, w_qkv, precision=highest))
    projected = projected.reshape(groups, length_seq, 3, HEADS, HEAD_DIM)
    cosine, sine = rotary_tables(length_seq)
    cosine = cosine[None, :, None, :]
    sine = sine[None, :, None, :]
    raw_query = projected[:, :, 0]
    raw_key = projected[:, :, 1]
    queries = low(raw_query * cosine + rotate_half(raw_query) * sine)
    keys = low(raw_key * cosine + rotate_half(raw_key) * sine)
    values = low(projected[:, :, 2])
    attended = attention(queries, keys, values)
    attended = low(low_back(attended)).reshape(groups, length_seq, D)
    branch = low_back(jnp.einsum('gld,de->gle', attended, w_out, precision=highest))
    after_attn = stream + branch
    normed_ffn = low(layer_norm(after_attn, gain_ffn))
    gate_up = low_back(jnp.einsum('gld,de->gle', normed_ffn, w_in, precision=highest))
    activated = low(jax.nn.gelu(gate_up[..., :FF], approximate=False) * gate_up[..., FF:])
    ffn_branch = low_back(jnp.einsum('glf,fd->gld', activated, w_down, precision=highest))
    return after_attn + ffn_branch

def reference(tokens, gain_attn, w_qkv, w_out, gain_ffn, w_in, w_down, cotangent):
    total_seqs = tokens.shape[0] // LENGTH
    group = math.gcd(total_seqs, max(1, 4096 // LENGTH))
    steps_count = total_seqs // group
    inputs = tokens.astype(jnp.float32).reshape(steps_count, group, LENGTH, D)
    cotangents = cotangent.astype(jnp.float32).reshape(steps_count, group, LENGTH, D)
    weights = tuple((w.astype(jnp.float32) for w in (gain_attn, w_qkv, w_out, gain_ffn, w_in, w_down)))

    def one_step(totals, pieces):
        inputs_part, cot_part = pieces
        result, pull = jax.vjp(forward, inputs_part, *weights)
        grads = pull(cot_part)
        totals = tuple((a + b for a, b in zip(totals, grads[1:])))
        return (totals, (result.astype(jnp.bfloat16), grads[0].astype(jnp.bfloat16)))
    zeros = tuple((jnp.zeros_like(w) for w in weights))
    totals, (results, input_grads) = lax.scan(one_step, zeros, (inputs, cotangents))
    return (results.reshape(tokens.shape[0], D), input_grads.reshape(tokens.shape[0], D), totals[0], totals[1], totals[2], totals[3], totals[4], totals[5])
```

```python
import functools

import jax
import jax.numpy as jnp
from jax import lax
from jax.experimental import pallas as pl
from jax.experimental.pallas import tpu as pltpu
from jax.sharding import PartitionSpec as P

D = 768
HEADS = 12
HEAD_DIM = 64
FF = 1152
WINDOW = 128
LENGTH = 1024
MARGIN = WINDOW // 2
QB = 128
SPAN = QB + 2 * MARGIN
PAIRS = D // 128
SCALE = HEAD_DIM ** (-0.5)
F32 = jnp.float32
BF16 = jnp.bfloat16
EPS = 1e-05
LIMIT = 60 * 1024 * 1024


def dot(a, b):
    return jnp.dot(a, b, preferred_element_type=F32)


def dot_nt(a, b):
    return lax.dot_general(a, b, (((1,), (1,)), ((), ())), preferred_element_type=F32)


def dot_tn(a, b):
    return lax.dot_general(a, b, (((0,), (0,)), ((), ())), preferred_element_type=F32)


def normalize(values):
    centre = values - jnp.mean(values, axis=-1, keepdims=True)
    inverse = lax.rsqrt(jnp.mean(centre * centre, axis=-1, keepdims=True) + EPS)
    return centre * inverse, inverse


def norm_back(grad_norm, standard, inverse, gain):
    scaled = grad_norm * gain
    return inverse * (
        scaled
        - jnp.mean(scaled, axis=-1, keepdims=True)
        - standard * jnp.mean(scaled * standard, axis=-1, keepdims=True)
    )


def rotary_tables(count):
    half_dim = HEAD_DIM // 2
    freqs = 10000.0 ** (-(jnp.arange(half_dim, dtype=F32) * 2.0) / HEAD_DIM)
    angles = jnp.arange(count, dtype=jnp.int32).astype(F32)[:, None] * freqs[None, :]
    cosine, sine = jnp.cos(angles), jnp.sin(angles)
    return (
        jnp.concatenate([cosine] * 4, axis=1),
        jnp.concatenate([-sine, sine, -sine, sine], axis=1),
    )


def swapped(u):
    lane = lax.broadcasted_iota(jnp.int32, u.shape, 1)
    return jnp.where((lane % 64) < 32, pltpu.roll(u, 96, 1), pltpu.roll(u, 32, 1))


def stack_heads(u):
    first = lax.broadcasted_iota(jnp.int32, u.shape, 1) < HEAD_DIM
    zero = jnp.zeros_like(u)
    return jnp.concatenate([jnp.where(first, u, zero), jnp.where(first, zero, u)], axis=0)


def merge_heads(u):
    top, low = u[:QB], u[QB:]
    first = lax.broadcasted_iota(jnp.int32, top.shape, 1) < HEAD_DIM
    return jnp.where(first, top, low)


def block_place(i):
    q_start = pl.multiple_of(i * QB, QB)
    k_start = pl.multiple_of(jnp.clip(i * QB - MARGIN, 0, LENGTH - SPAN), MARGIN)
    row = lax.broadcasted_iota(jnp.int32, (2 * QB, SPAN), 0)
    col = lax.broadcasted_iota(jnp.int32, (2 * QB, SPAN), 1)
    allowed = jnp.abs(q_start + (row % QB) - (k_start + col)) <= MARGIN
    return q_start, k_start, allowed


def softmax(queries, keys, allowed):
    scores = jnp.where(allowed, dot_nt(queries, keys), -1e30)
    expo = jnp.exp(scores - jnp.max(scores, axis=-1, keepdims=True))
    return expo * (1.0 / jnp.sum(expo, axis=-1, keepdims=True))


def attend_kernel(x_ref, gain_ref, w_ref, cos_ref, sin_ref, q_ref, k_ref, v_ref, att_ref):
    chunk = 256

    @pl.loop(0, LENGTH // chunk)
    def _(c):
        rows = pl.ds(pl.multiple_of(c * chunk, chunk), chunk)
        standard, _ = normalize(x_ref[rows, :].astype(F32))
        normed = (standard * gain_ref[...]).astype(BF16)
        cosine, sine = cos_ref[rows, :], sin_ref[rows, :]
        for part, ref in ((0, q_ref), (1, k_ref)):
            raw = dot(normed, w_ref[:, part * D : (part + 1) * D])
            for g in range(PAIRS):
                u = raw[:, g * 128 : (g + 1) * 128]
                ref[rows, g * 128 : (g + 1) * 128] = (u * cosine + swapped(u) * sine).astype(BF16)
        v_ref[rows, :] = dot(normed, w_ref[:, 2 * D :]).astype(BF16)

    @pl.loop(0, LENGTH // QB)
    def _(i):
        q_start, k_start, allowed = block_place(i)
        for g in range(PAIRS):
            lanes = slice(g * 128, (g + 1) * 128)
            queries = stack_heads(q_ref[pl.ds(q_start, QB), lanes] * SCALE)
            probs = softmax(queries, k_ref[pl.ds(k_start, SPAN), lanes], allowed)
            mixed = dot(probs.astype(BF16), v_ref[pl.ds(k_start, SPAN), lanes])
            att_ref[pl.ds(q_start, QB), lanes] = merge_heads(mixed).astype(BF16)


def column_of(row):
    return jnp.transpose(jnp.broadcast_to(row, (128, D)))


def ffn_kernel(
    x_ref, att_ref, cot_ref, gain_ref, wo_ref, wi_ref, wd_ref,
    out_ref, after_ref, gatt_ref, gout_ref, gin_ref, gdown_ref,
    out_acc, in_acc, down_acc, gain_acc,
):
    step = pl.program_id(0)

    @pl.when(step == 0)
    def _():
        out_acc[...] = jnp.zeros_like(out_acc)
        in_acc[...] = jnp.zeros_like(in_acc)
        down_acc[...] = jnp.zeros_like(down_acc)
        gain_acc[...] = jnp.zeros_like(gain_acc)

    att = att_ref[...]
    cot = cot_ref[...]
    gain = gain_ref[...]
    after = x_ref[...].astype(F32) + dot(att, wo_ref[...])
    standard, inverse = normalize(after)
    normed = (standard * gain).astype(BF16)
    lifted = dot(normed, wi_ref[:, :FF])
    gate = dot(normed, wi_ref[:, FF:])
    grad_act = dot_nt(cot, wd_ref[...])
    cdf = 0.5 * (1.0 + lax.erf(lifted * 0.7071067811865476))
    gelu = lifted * cdf
    activated = (gelu * gate).astype(BF16)
    density = jnp.exp(-0.5 * lifted * lifted) * 0.3989422804014327
    grad_lifted = (grad_act * gate * (cdf + lifted * density)).astype(BF16)
    grad_gate = (grad_act * gelu).astype(BF16)
    out_ref[...] = (after + dot(activated, wd_ref[...])).astype(BF16)
    down_acc[...] += dot_tn(activated, cot)
    in_acc[:, :FF] += dot_tn(normed, grad_lifted)
    in_acc[:, FF:] += dot_tn(normed, grad_gate)
    grad_norm = dot_nt(grad_lifted, wi_ref[:, :FF]) + dot_nt(grad_gate, wi_ref[:, FF:])
    gain_acc[...] += jnp.sum(grad_norm * standard, axis=0, keepdims=True)
    grad_after = cot.astype(F32) + norm_back(grad_norm, standard, inverse, gain)
    after_ref[...] = grad_after
    branch = grad_after.astype(BF16)
    out_acc[...] += dot_tn(att, branch)
    gatt_ref[...] = dot_nt(branch, wo_ref[...]).astype(BF16)

    @pl.when(step == pl.num_programs(0) - 1)
    def _():
        for h in range(2):
            gout_ref[h] = out_acc[:, h * (D // 2) : (h + 1) * (D // 2)].astype(BF16)
            gdown_ref[h] = down_acc[:, h * (D // 2) : (h + 1) * (D // 2)].astype(BF16)
            gin_ref[h, :, :FF] = in_acc[:, h * FF : (h + 1) * FF].astype(BF16)
            gin_ref[h, :, FF:] = column_of(gain_acc[...]).astype(BF16)


def back_kernel(
    q_ref, k_ref, v_ref, gatt_ref, cos_ref, sin_ref, gp_ref, dk_ref, dv_ref
):
    dk_ref[...] = jnp.zeros_like(dk_ref)
    dv_ref[...] = jnp.zeros_like(dv_ref)

    @pl.loop(0, LENGTH // QB)
    def _(i):
        q_start, k_start, allowed = block_place(i)
        q_rows, k_rows = pl.ds(q_start, QB), pl.ds(k_start, SPAN)
        cosine, sine = cos_ref[q_rows, :], sin_ref[q_rows, :]
        for g in range(PAIRS):
            lanes = slice(g * 128, (g + 1) * 128)
            queries = stack_heads(q_ref[q_rows, lanes] * SCALE)
            keys = k_ref[k_rows, lanes]
            grads = stack_heads(gatt_ref[q_rows, lanes])
            probs = softmax(queries, keys, allowed)
            grad_probs = dot_nt(grads, v_ref[k_rows, lanes])
            centre = jnp.sum(grad_probs * probs, axis=-1, keepdims=True)
            grad_scores = (probs * (grad_probs - centre)).astype(BF16)
            u = merge_heads(dot(grad_scores, keys)) * SCALE
            gp_ref[q_rows, lanes] = (u * cosine - swapped(u) * sine).astype(BF16)
            dk_ref[k_rows, lanes] += dot_tn(grad_scores, queries)
            dv_ref[k_rows, lanes] += dot_tn(probs.astype(BF16), grads)

    chunk = 256

    @pl.loop(0, LENGTH // chunk)
    def _(c):
        rows = pl.ds(pl.multiple_of(c * chunk, chunk), chunk)
        cosine, sine = cos_ref[rows, :], sin_ref[rows, :]
        for g in range(PAIRS):
            u = dk_ref[rows, g * 128 : (g + 1) * 128]
            gp_ref[rows, D + g * 128 : D + (g + 1) * 128] = (
                u * cosine - swapped(u) * sine
            ).astype(BF16)
        gp_ref[rows, 2 * D :] = dv_ref[rows, :].astype(BF16)


def last_kernel(
    x_ref, after_ref, gp_ref, gain_ref, w_ref, ig_ref, gq_ref, acc, gain_acc
):
    step = pl.program_id(0)

    @pl.when(step == 0)
    def _():
        acc[...] = jnp.zeros_like(acc)
        gain_acc[...] = jnp.zeros_like(gain_acc)

    gain = gain_ref[...]
    standard, inverse = normalize(x_ref[...].astype(F32))
    normed = (standard * gain).astype(BF16)
    grad_projected = gp_ref[...]
    acc[...] += dot_tn(normed, grad_projected)
    grad_norm = dot_nt(grad_projected, w_ref[...])
    gain_acc[...] += jnp.sum(grad_norm * standard, axis=0, keepdims=True)
    ig_ref[...] = (after_ref[...] + norm_back(grad_norm, standard, inverse, gain)).astype(BF16)

    @pl.when(step == pl.num_programs(0) - 1)
    def _():
        for h in range(2):
            gq_ref[h, :, :FF] = acc[:, h * FF : (h + 1) * FF].astype(BF16)
            gq_ref[h, :, FF:] = column_of(gain_acc[...]).astype(BF16)


def shape(dims, dtype):
    return jax.ShapeDtypeStruct(dims, dtype)


def cost(flops, bytes_accessed):
    return pl.CostEstimate(flops=flops, bytes_accessed=bytes_accessed, transcendentals=0)


PARAMS = pltpu.CompilerParams(vmem_limit_bytes=LIMIT)
WHOLE = pl.BlockSpec(memory_space=pltpu.VMEM)
ROWS = 256


def by_rows(width):
    return pl.BlockSpec((ROWS, width), lambda i: (i, 0))


def fixed(*dims):
    return pl.BlockSpec(dims, lambda i: (0,) * len(dims), pipeline_mode=pl.Buffered(1))


def attend(x, gain, w, cosine, sine):
    t = x.shape[0]
    return pl.pallas_call(
        attend_kernel,
        out_shape=[shape((t, D), BF16)] * 4,
        in_specs=[WHOLE] * 5,
        out_specs=[WHOLE] * 4,
        compiler_params=PARAMS,
        cost_estimate=cost(8_000_000_000, 14_000_000),
        name="attend",
    )(x, gain, w, cosine, sine)


def ffn(x, att, cot, gain, wo, wi, wd):
    t = x.shape[0]
    return pl.pallas_call(
        ffn_kernel,
        grid=(t // ROWS,),
        in_specs=[
            by_rows(D), by_rows(D), by_rows(D), fixed(1, D),
            fixed(D, D), fixed(D, 2 * FF), fixed(FF, D),
        ],
        out_specs=[
            by_rows(D), by_rows(D), by_rows(D),
            fixed(2, D, D // 2), fixed(2, D, FF + 128), fixed(2, FF, D // 2),
        ],
        out_shape=[
            shape((t, D), BF16), shape((t, D), F32), shape((t, D), BF16),
            shape((2, D, D // 2), BF16), shape((2, D, FF + 128), BF16), shape((2, FF, D // 2), BF16),
        ],
        scratch_shapes=[
            pltpu.VMEM((D, D), F32), pltpu.VMEM((D, 2 * FF), F32),
            pltpu.VMEM((FF, D), F32), pltpu.VMEM((1, D), F32),
        ],
        compiler_params=PARAMS,
        cost_estimate=cost(20_000_000_000, 25_000_000),
        name="ffn",
    )(x, att, cot, gain, wo, wi, wd)


def back(q, k, v, gatt, cosine, sine):
    t = q.shape[0]
    return pl.pallas_call(
        back_kernel,
        out_shape=shape((t, 3 * D), BF16),
        in_specs=[WHOLE] * 6,
        out_specs=WHOLE,
        scratch_shapes=[pltpu.VMEM((t, D), F32), pltpu.VMEM((t, D), F32)],
        compiler_params=PARAMS,
        cost_estimate=cost(10_000_000_000, 14_000_000),
        name="back",
    )(q, k, v, gatt, cosine, sine)


def last(x, after, gp, gain, w):
    t = x.shape[0]
    return pl.pallas_call(
        last_kernel,
        grid=(t // ROWS,),
        in_specs=[by_rows(D), by_rows(D), by_rows(3 * D), fixed(1, D), fixed(D, 3 * D)],
        out_specs=[by_rows(D), fixed(2, D, FF + 128)],
        out_shape=[shape((t, D), BF16), shape((2, D, FF + 128), BF16)],
        scratch_shapes=[pltpu.VMEM((D, 3 * D), F32), pltpu.VMEM((1, D), F32)],
        compiler_params=PARAMS,
        cost_estimate=cost(8_000_000_000, 20_000_000),
        name="last",
    )(x, after, gp, gain, w)


def body(copies, tokens, gain_attn, w_qkv, w_out, gain_ffn, w_in, w_down, cotangent):
    core = lax.axis_index("replica") % 2
    to_core = [(r, r ^ 1) for r in range(copies)]
    to_chip = [(r, r ^ 2) for r in range(copies)]

    def in_order(mine, other):
        return jnp.concatenate(
            [jnp.where(core == 0, mine, other), jnp.where(core == 0, other, mine)], axis=1
        )

    def half_of(w):
        width = w.shape[1] // 2
        return lax.dynamic_slice_in_dim(w, core * width, width, 1)

    def gather(w):
        mine = lax.all_gather(w, "shard", axis=0, tiled=True)
        return mine, lax.ppermute(mine, "replica", to_core)

    def reduce_rows(g):
        mine = lax.dynamic_index_in_dim(g, core, 0, keepdims=False)
        theirs = lax.dynamic_index_in_dim(g, 1 - core, 0, keepdims=False)
        theirs = lax.ppermute(theirs, "replica", to_core)
        part = (mine.astype(F32) + theirs.astype(F32)).astype(BF16)
        part = lax.psum_scatter(part, "shard", scatter_dimension=0, tiled=True)
        for perm in () if copies < 4 else (to_chip,):
            across = lax.ppermute(part, "replica", perm)
            part = (part.astype(F32) + across.astype(F32)).astype(BF16)
        other = lax.ppermute(part, "replica", to_core)
        return part.astype(F32), other.astype(F32)

    gains = jnp.stack([gain_attn, gain_ffn], axis=1)
    gains = jnp.pad(gains, ((0, 0), (0, 126)))
    mine, other = gather(jnp.concatenate([half_of(w_qkv), gains], axis=1))
    joint = in_order(mine[:, :FF], other[:, :FF])
    gain_one = mine[:, FF].astype(F32)[None, :]
    gain_two = mine[:, FF + 1].astype(F32)[None, :]
    out_weight = in_order(*gather(half_of(w_out)))
    in_weight = in_order(*gather(half_of(w_in)))
    down_weight = in_order(*gather(half_of(w_down)))

    cosine, sine = rotary_tables(LENGTH)
    q, k, v, att = attend(tokens, gain_one, joint, cosine, sine)
    output, after, gatt, gout, gin, gdown = ffn(
        tokens, att, cotangent, gain_two, out_weight, in_weight, down_weight
    )
    gp = back(q, k, v, gatt, cosine, sine)
    input_grad, gqkv = last(tokens, after, gp, gain_one, joint)

    in_mine, in_other = reduce_rows(gin)
    grad_down = in_order(*reduce_rows(gdown))
    grad_out = in_order(*reduce_rows(gout))
    qkv_mine, qkv_other = reduce_rows(gqkv)
    return (
        output,
        input_grad,
        qkv_mine[:, FF],
        in_order(qkv_mine[:, :FF], qkv_other[:, :FF]),
        grad_out,
        in_mine[:, FF],
        in_order(in_mine[:, :FF], in_other[:, :FF]),
        grad_down,
    )


def solution(mesh):
    return jax.shard_map(
        functools.partial(body, mesh.shape["replica"]),
        mesh=mesh,
        in_specs=(
            P(("replica", "shard"), None),
            P("shard"),
            P("shard", None),
            P("shard", None),
            P("shard"),
            P("shard", None),
            P("shard", None),
            P(("replica", "shard"), None),
        ),
        out_specs=(
            P(("replica", "shard"), None),
            P(("replica", "shard"), None),
            P("shard"),
            P("shard", None),
            P("shard", None),
            P("shard"),
            P("shard", None),
            P("shard", None),
        ),
        check_vma=False,
    )
```

```python
import functools

import jax
import jax.numpy as jnp
from jax import lax
from jax.experimental import pallas as pl
from jax.experimental.pallas import tpu as pltpu
from jax.sharding import PartitionSpec as P

D = 768
HEADS = 12
HEAD_DIM = 64
FF = 1152
WINDOW = 128
LENGTH = 1024
MARGIN = WINDOW // 2
QB = 128
SPAN = QB + 2 * MARGIN
PAIRS = D // 128
SCALE = HEAD_DIM ** (-0.5)
F32 = jnp.float32
BF16 = jnp.bfloat16
EPS = 1e-05
LIMIT = 60 * 1024 * 1024


def dot(a, b):
    return jnp.dot(a, b, preferred_element_type=F32)


def dot_nt(a, b):
    return lax.dot_general(a, b, (((1,), (1,)), ((), ())), preferred_element_type=F32)


def dot_tn(a, b):
    return lax.dot_general(a, b, (((0,), (0,)), ((), ())), preferred_element_type=F32)


def normalize(values):
    centre = values - jnp.mean(values, axis=-1, keepdims=True)
    inverse = lax.rsqrt(jnp.mean(centre * centre, axis=-1, keepdims=True) + EPS)
    return centre * inverse, inverse


def norm_back(grad_norm, standard, inverse, gain):
    scaled = grad_norm * gain
    return inverse * (
        scaled
        - jnp.mean(scaled, axis=-1, keepdims=True)
        - standard * jnp.mean(scaled * standard, axis=-1, keepdims=True)
    )


def rotary_tables(count):
    half_dim = HEAD_DIM // 2
    freqs = 10000.0 ** (-(jnp.arange(half_dim, dtype=F32) * 2.0) / HEAD_DIM)
    angles = jnp.arange(count, dtype=jnp.int32).astype(F32)[:, None] * freqs[None, :]
    cosine, sine = jnp.cos(angles), jnp.sin(angles)
    return (
        jnp.concatenate([cosine] * 4, axis=1),
        jnp.concatenate([-sine, sine, -sine, sine], axis=1),
    )


def swapped(u):
    lane = lax.broadcasted_iota(jnp.int32, u.shape, 1)
    return jnp.where((lane % 64) < 32, pltpu.roll(u, 96, 1), pltpu.roll(u, 32, 1))


def stack_heads(u):
    first = lax.broadcasted_iota(jnp.int32, u.shape, 1) < HEAD_DIM
    zero = jnp.zeros_like(u)
    return jnp.concatenate([jnp.where(first, u, zero), jnp.where(first, zero, u)], axis=0)


def merge_heads(u):
    top, low = u[:QB], u[QB:]
    first = lax.broadcasted_iota(jnp.int32, top.shape, 1) < HEAD_DIM
    return jnp.where(first, top, low)


def block_place(i):
    q_start = pl.multiple_of(i * QB, QB)
    k_start = pl.multiple_of(jnp.clip(i * QB - MARGIN, 0, LENGTH - SPAN), MARGIN)
    row = lax.broadcasted_iota(jnp.int32, (2 * QB, SPAN), 0)
    col = lax.broadcasted_iota(jnp.int32, (2 * QB, SPAN), 1)
    allowed = jnp.abs(q_start + (row % QB) - (k_start + col)) <= MARGIN
    return q_start, k_start, allowed


def softmax(queries, keys, allowed):
    scores = jnp.where(allowed, dot_nt(queries, keys), -1e30)
    expo = jnp.exp(scores - jnp.max(scores, axis=-1, keepdims=True))
    return expo * (1.0 / jnp.sum(expo, axis=-1, keepdims=True))


def attend_kernel(x_ref, gain_ref, w_ref, cos_ref, sin_ref, q_ref, k_ref, v_ref, att_ref):
    chunk = 256

    @pl.loop(0, LENGTH // chunk)
    def _(c):
        rows = pl.ds(pl.multiple_of(c * chunk, chunk), chunk)
        standard, _ = normalize(x_ref[rows, :].astype(F32))
        normed = (standard * gain_ref[...]).astype(BF16)
        cosine, sine = cos_ref[rows, :], sin_ref[rows, :]
        for part, ref in ((0, q_ref), (1, k_ref)):
            raw = dot(normed, w_ref[:, part * D : (part + 1) * D])
            for g in range(PAIRS):
                u = raw[:, g * 128 : (g + 1) * 128]
                ref[rows, g * 128 : (g + 1) * 128] = (u * cosine + swapped(u) * sine).astype(BF16)
        v_ref[rows, :] = dot(normed, w_ref[:, 2 * D :]).astype(BF16)

    @pl.loop(0, LENGTH // QB)
    def _(i):
        q_start, k_start, allowed = block_place(i)
        for g in range(PAIRS):
            lanes = slice(g * 128, (g + 1) * 128)
            queries = stack_heads(q_ref[pl.ds(q_start, QB), lanes] * SCALE)
            probs = softmax(queries, k_ref[pl.ds(k_start, SPAN), lanes], allowed)
            mixed = dot(probs.astype(BF16), v_ref[pl.ds(k_start, SPAN), lanes])
            att_ref[pl.ds(q_start, QB), lanes] = merge_heads(mixed).astype(BF16)


def column_of(row):
    return jnp.transpose(jnp.broadcast_to(row, (128, D)))


def ffn_kernel(
    x_ref, att_ref, cot_ref, gain_ref, wo_ref, wi_ref, wd_ref,
    out_ref, after_ref, gatt_ref, gout_ref, gin_ref, gdown_ref,
    out_acc, in_acc, down_acc, gain_acc,
):
    step = pl.program_id(0)

    @pl.when(step == 0)
    def _():
        out_acc[...] = jnp.zeros_like(out_acc)
        in_acc[...] = jnp.zeros_like(in_acc)
        down_acc[...] = jnp.zeros_like(down_acc)
        gain_acc[...] = jnp.zeros_like(gain_acc)

    att = att_ref[...]
    cot = cot_ref[...]
    gain = gain_ref[...]
    after = x_ref[...].astype(F32) + dot(att, wo_ref[...])
    standard, inverse = normalize(after)
    normed = (standard * gain).astype(BF16)
    lifted = dot(normed, wi_ref[:, :FF])
    gate = dot(normed, wi_ref[:, FF:])
    grad_act = dot_nt(cot, wd_ref[...])
    cdf = 0.5 * (1.0 + lax.erf(lifted * 0.7071067811865476))
    gelu = lifted * cdf
    activated = (gelu * gate).astype(BF16)
    density = jnp.exp(-0.5 * lifted * lifted) * 0.3989422804014327
    grad_lifted = (grad_act * gate * (cdf + lifted * density)).astype(BF16)
    grad_gate = (grad_act * gelu).astype(BF16)
    out_ref[...] = (after + dot(activated, wd_ref[...])).astype(BF16)
    down_acc[...] += dot_tn(activated, cot)
    in_acc[:, :FF] += dot_tn(normed, grad_lifted)
    in_acc[:, FF:] += dot_tn(normed, grad_gate)
    grad_norm = dot_nt(grad_lifted, wi_ref[:, :FF]) + dot_nt(grad_gate, wi_ref[:, FF:])
    gain_acc[...] += jnp.sum(grad_norm * standard, axis=0, keepdims=True)
    grad_after = cot.astype(F32) + norm_back(grad_norm, standard, inverse, gain)
    after_ref[...] = grad_after
    branch = grad_after.astype(BF16)
    out_acc[...] += dot_tn(att, branch)
    gatt_ref[...] = dot_nt(branch, wo_ref[...]).astype(BF16)

    @pl.when(step == pl.num_programs(0) - 1)
    def _():
        for h in range(2):
            gout_ref[h] = out_acc[:, h * (D // 2) : (h + 1) * (D // 2)].astype(BF16)
            gdown_ref[h] = down_acc[:, h * (D // 2) : (h + 1) * (D // 2)].astype(BF16)
            gin_ref[h, :, :FF] = in_acc[:, h * FF : (h + 1) * FF].astype(BF16)
            gin_ref[h, :, FF:] = column_of(gain_acc[...]).astype(BF16)


def back_kernel(
    q_ref, k_ref, v_ref, gatt_ref, cos_ref, sin_ref, gp_ref, dk_ref, dv_ref
):
    dk_ref[...] = jnp.zeros_like(dk_ref)
    dv_ref[...] = jnp.zeros_like(dv_ref)

    @pl.loop(0, LENGTH // QB)
    def _(i):
        q_start, k_start, allowed = block_place(i)
        q_rows, k_rows = pl.ds(q_start, QB), pl.ds(k_start, SPAN)
        cosine, sine = cos_ref[q_rows, :], sin_ref[q_rows, :]
        for g in range(PAIRS):
            lanes = slice(g * 128, (g + 1) * 128)
            queries = stack_heads(q_ref[q_rows, lanes] * SCALE)
            keys = k_ref[k_rows, lanes]
            grads = stack_heads(gatt_ref[q_rows, lanes])
            probs = softmax(queries, keys, allowed)
            grad_probs = dot_nt(grads, v_ref[k_rows, lanes])
            centre = jnp.sum(grad_probs * probs, axis=-1, keepdims=True)
            grad_scores = (probs * (grad_probs - centre)).astype(BF16)
            u = merge_heads(dot(grad_scores, keys)) * SCALE
            gp_ref[q_rows, lanes] = (u * cosine - swapped(u) * sine).astype(BF16)
            dk_ref[k_rows, lanes] += dot_tn(grad_scores, queries)
            dv_ref[k_rows, lanes] += dot_tn(probs.astype(BF16), grads)

    chunk = 256

    @pl.loop(0, LENGTH // chunk)
    def _(c):
        rows = pl.ds(pl.multiple_of(c * chunk, chunk), chunk)
        cosine, sine = cos_ref[rows, :], sin_ref[rows, :]
        for g in range(PAIRS):
            u = dk_ref[rows, g * 128 : (g + 1) * 128]
            gp_ref[rows, D + g * 128 : D + (g + 1) * 128] = (
                u * cosine - swapped(u) * sine
            ).astype(BF16)
        gp_ref[rows, 2 * D :] = dv_ref[rows, :].astype(BF16)


def last_kernel(
    x_ref, after_ref, gp_ref, gain_ref, w_ref, ig_ref, gq_ref, acc, gain_acc
):
    step = pl.program_id(0)

    @pl.when(step == 0)
    def _():
        acc[...] = jnp.zeros_like(acc)
        gain_acc[...] = jnp.zeros_like(gain_acc)

    gain = gain_ref[...]
    standard, inverse = normalize(x_ref[...].astype(F32))
    normed = (standard * gain).astype(BF16)
    grad_projected = gp_ref[...]
    acc[...] += dot_tn(normed, grad_projected)
    grad_norm = dot_nt(grad_projected, w_ref[...])
    gain_acc[...] += jnp.sum(grad_norm * standard, axis=0, keepdims=True)
    ig_ref[...] = (after_ref[...] + norm_back(grad_norm, standard, inverse, gain)).astype(BF16)

    @pl.when(step == pl.num_programs(0) - 1)
    def _():
        for h in range(2):
            gq_ref[h, :, :FF] = acc[:, h * FF : (h + 1) * FF].astype(BF16)
            gq_ref[h, :, FF:] = column_of(gain_acc[...]).astype(BF16)


def shape(dims, dtype):
    return jax.ShapeDtypeStruct(dims, dtype)


def cost(flops, bytes_accessed):
    return pl.CostEstimate(flops=flops, bytes_accessed=bytes_accessed, transcendentals=0)


PARAMS = pltpu.CompilerParams(vmem_limit_bytes=LIMIT)
WHOLE = pl.BlockSpec(memory_space=pltpu.VMEM)
ROWS = 256


def by_rows(width):
    return pl.BlockSpec((ROWS, width), lambda i: (i, 0))


def fixed(*dims):
    return pl.BlockSpec(dims, lambda i: (0,) * len(dims), pipeline_mode=pl.Buffered(1))


def attend(x, gain, w, cosine, sine):
    t = x.shape[0]
    return pl.pallas_call(
        attend_kernel,
        out_shape=[shape((t, D), BF16)] * 4,
        in_specs=[WHOLE] * 5,
        out_specs=[WHOLE] * 4,
        compiler_params=PARAMS,
        cost_estimate=cost(23_000_000_000, 14_000_000),
        name="attend",
    )(x, gain, w, cosine, sine)


def ffn(x, att, cot, gain, wo, wi, wd):
    t = x.shape[0]
    return pl.pallas_call(
        ffn_kernel,
        grid=(t // ROWS,),
        in_specs=[
            by_rows(D), by_rows(D), by_rows(D), fixed(1, D),
            fixed(D, D), fixed(D, 2 * FF), fixed(FF, D),
        ],
        out_specs=[
            by_rows(D), by_rows(D), by_rows(D),
            fixed(2, D, D // 2), fixed(2, D, FF + 128), fixed(2, FF, D // 2),
        ],
        out_shape=[
            shape((t, D), BF16), shape((t, D), F32), shape((t, D), BF16),
            shape((2, D, D // 2), BF16), shape((2, D, FF + 128), BF16), shape((2, FF, D // 2), BF16),
        ],
        scratch_shapes=[
            pltpu.VMEM((D, D), F32), pltpu.VMEM((D, 2 * FF), F32),
            pltpu.VMEM((FF, D), F32), pltpu.VMEM((1, D), F32),
        ],
        compiler_params=PARAMS,
        cost_estimate=cost(41_000_000_000, 25_000_000),
        name="ffn",
    )(x, att, cot, gain, wo, wi, wd)


def back(q, k, v, gatt, cosine, sine):
    t = q.shape[0]
    return pl.pallas_call(
        back_kernel,
        out_shape=shape((t, 3 * D), BF16),
        in_specs=[WHOLE] * 6,
        out_specs=WHOLE,
        scratch_shapes=[pltpu.VMEM((t, D), F32), pltpu.VMEM((t, D), F32)],
        compiler_params=PARAMS,
        cost_estimate=cost(41_000_000_000, 14_000_000),
        name="back",
    )(q, k, v, gatt, cosine, sine)


def last(x, after, gp, gain, w):
    t = x.shape[0]
    return pl.pallas_call(
        last_kernel,
        grid=(t // ROWS,),
        in_specs=[by_rows(D), by_rows(D), by_rows(3 * D), fixed(1, D), fixed(D, 3 * D)],
        out_specs=[by_rows(D), fixed(2, D, FF + 128)],
        out_shape=[shape((t, D), BF16), shape((2, D, FF + 128), BF16)],
        scratch_shapes=[pltpu.VMEM((D, 3 * D), F32), pltpu.VMEM((1, D), F32)],
        compiler_params=PARAMS,
        cost_estimate=cost(18_000_000_000, 20_000_000),
        name="last",
    )(x, after, gp, gain, w)


def add(a, b):
    return (a.astype(F32) + b.astype(F32)).astype(BF16)


def body(copies, shards, tokens, gain_attn, w_qkv, w_out, gain_ffn, w_in, w_down, cotangent):
    core = lax.axis_index("replica") % 2
    to_core = [(r, r ^ 1) for r in range(copies)]
    to_chip = [(r, r ^ 2) for r in range(copies)]

    def in_order(mine, other):
        return jnp.concatenate(
            [jnp.where(core == 0, mine, other), jnp.where(core == 0, other, mine)], axis=1
        )

    def half_of(w):
        width = w.shape[1] // 2
        return lax.dynamic_slice_in_dim(w, core * width, width, 1)

    place = lax.axis_index("shard")
    bits = shards.bit_length() - 1

    def across(w, bit):
        return lax.ppermute(w, "shard", [(i, i ^ (1 << bit)) for i in range(shards)])

    def my_bit(bit):
        return (place // (1 << bit)) % 2

    def widen(w, bit):
        other = across(w, bit)
        low = my_bit(bit) == 0
        return jnp.stack([jnp.where(low, w, other), jnp.where(low, other, w)], axis=-3)

    def join(w, other):
        low = my_bit(0) == 0
        w = jnp.stack([jnp.where(low, w, other), jnp.where(low, other, w)], axis=-3)
        w = w.reshape(-1, w.shape[-1])
        return w, lax.ppermute(w, "replica", to_core)

    def over_core(g):
        rows, width = g.shape[1] // shards, g.shape[2]
        mine = lax.dynamic_index_in_dim(g, core, 0, keepdims=False)
        theirs = lax.dynamic_index_in_dim(g, 1 - core, 0, keepdims=False)
        theirs = lax.ppermute(theirs, "replica", to_core)
        return add(mine, theirs).reshape(shards, rows, width)

    def over_bit(part, bit):
        pairs = part.reshape((-1, 2) + part.shape[1:])
        mine = lax.dynamic_index_in_dim(pairs, my_bit(bit), 1, keepdims=False)
        theirs = lax.dynamic_index_in_dim(pairs, 1 - my_bit(bit), 1, keepdims=False)
        return add(mine, across(theirs, bit))

    def settle(part, done):
        for bit in range(done, bits):
            part = over_bit(part, bit)
        part = part[0]
        if copies == 4:
            part = add(part, lax.ppermute(part, "replica", to_chip))
        other = lax.ppermute(part, "replica", to_core)
        return part.astype(F32), other.astype(F32)

    gains = jnp.stack([gain_attn, gain_ffn], axis=1)
    gains = jnp.pad(gains, ((0, 0), (0, 126)))
    first = jnp.concatenate([half_of(w_qkv), gains], axis=1)
    for bit in range(bits - 1, 0, -1):
        first = widen(first, bit)
    first, *rest = lax.optimization_barrier(
        (first, half_of(w_in), half_of(w_down), half_of(w_out))
    )
    mine, other = join(first, across(first, 0))
    for bit in range(bits - 1, 0, -1):
        rest = [widen(w, bit) for w in rest]
    joint = in_order(mine[:, :FF], other[:, :FF])
    gain_one = mine[:, FF].astype(F32)[None, :]
    gain_two = mine[:, FF + 1].astype(F32)[None, :]

    cosine, sine = rotary_tables(LENGTH)
    joint, *rest = lax.optimization_barrier((joint, *rest))
    arriving = [across(w, 0) for w in rest]
    q, k, v, att = attend(tokens, gain_one, joint, cosine, sine)
    att, *arriving = lax.optimization_barrier((att, *arriving))
    in_weight, down_weight, out_weight = (
        in_order(*join(w, other)) for w, other in zip(rest, arriving)
    )
    output, after, gatt, gout, gin, gdown = ffn(
        tokens, att, cotangent, gain_two, out_weight, in_weight, down_weight
    )
    parts = [over_core(g) for g in (gin, gdown, gout)]
    gatt, *parts = lax.optimization_barrier((gatt, *parts))
    gp = back(q, k, v, gatt, cosine, sine)
    parts = [over_bit(part, 0) for part in parts]
    gp, *parts = lax.optimization_barrier((gp, *parts))
    input_grad, gqkv = last(tokens, after, gp, gain_one, joint)
    parts = [over_bit(part, 1) for part in parts]
    gqkv, *parts = lax.optimization_barrier((gqkv, *parts))

    qkv_mine, qkv_other = settle(over_core(gqkv), 0)
    in_mine, in_other = settle(parts[0], 2)
    grad_down = in_order(*settle(parts[1], 2))
    grad_out = in_order(*settle(parts[2], 2))
    return (
        output,
        input_grad,
        qkv_mine[:, FF],
        in_order(qkv_mine[:, :FF], qkv_other[:, :FF]),
        grad_out,
        in_mine[:, FF],
        in_order(in_mine[:, :FF], in_other[:, :FF]),
        grad_down,
    )


def solution(mesh):
    return jax.shard_map(
        functools.partial(body, mesh.shape["replica"], mesh.shape["shard"]),
        mesh=mesh,
        in_specs=(
            P(("replica", "shard"), None),
            P("shard"),
            P("shard", None),
            P("shard", None),
            P("shard"),
            P("shard", None),
            P("shard", None),
            P(("replica", "shard"), None),
        ),
        out_specs=(
            P(("replica", "shard"), None),
            P(("replica", "shard"), None),
            P("shard"),
            P("shard", None),
            P("shard", None),
            P("shard"),
            P("shard", None),
            P("shard", None),
        ),
        check_vma=False,
    )
```
